32 devices in a mesh: group: 2 (over y), expert: 4 (over z), tensor: 4 (over x, core).
Axes of the slice: x: 2, y: 2, z: 4, core: 2. Of those that a mesh axis runs over, the one named last changes fastest.
Arguments:
- activations: bfloat16 [1024, 7168], P(('group', 'expert'), 'tensor'), parts along dimension 0, may hold values from -6 to 6
- out_grad: bfloat16 [1024, 7168], P(('group', 'expert'), 'tensor'), parts along dimension 0, may hold values from -6 to 6
- routes: int32 [1024, 2], P(('group', 'expert')), parts along dimension 0, may hold values from 0 to 3, all different within a row; in each aligned block of 128 rows (0 to 127, 128 to 255, ...) at most 96 rows name the same one
- gates: float32 [1024, 2], P(('group', 'expert')), parts along dimension 0, may hold values from 0.1 to 1
- gate_weight: bfloat16 [4, 7168, 2048], P('expert', None, 'tensor'), may hold values from -0.0625 to 0.0625
- up_weight: bfloat16 [4, 7168, 2048], P('expert', None, 'tensor'), may hold values from -0.0625 to 0.0625
- down_weight: bfloat16 [4, 2048, 7168], P('expert', 'tensor'), may hold values from -0.125 to 0.125
Outputs:
- input_grad: bfloat16 [1024, 7168], P(('group', 'expert'), 'tensor'), parts along dimension 0
The draws below stay inside these ranges and needn't reach their ends.
There are 2 independent parts, one for each index of `group`. The reference program is written for one: setup_inputs(seed, part) draws one part's arguments, and reference() takes and returns one part's arrays. A program takes and returns all parts, laid end to end along the dimension named above; an argument that names none is the same for every part. Nothing has to cross between parts.
Inputs may be any that keep to these rules, and one draw needn't show every extreme that they name: `routes`: each row names 2 different experts. Among the 128 rows of one index of expert no expert is named by more than 96 rows, a bound that some block reaches of them. Every expert is named by some row.
All inputs are finite; a program needn't handle non-finite values.
Results may differ from the reference program's by a relative error of at most 0.011.
Values may be sent and summed in bfloat16 or wider, within the bound.
A program may use at most 128 MiB of HBM per device.

```python
import math
import jax
import jax.numpy as jnp
import numpy as np
from jax import lax

D = 7168
FF = 2048
TOK_DEV = 128
TOP = 2
EXPERTS = 4
TOKENS = 512
CAP = 96
N_TENSOR = 4


def shard_levels(rng, extent, pieces, low, largest):
    factor_of = 1.0
    for dim, blocks in pieces:
        heights = jax.random.uniform(jax.random.fold_in(jax.random.fold_in(rng, 6), dim), (blocks,), jnp.float32, low / len(pieces), largest / len(pieces))
        factor_of = factor_of * jnp.repeat(jnp.exp(heights), extent[dim] // blocks).reshape((-1,) + (1,) * (len(extent) - 1 - dim))
    return factor_of


def shared_out(stream_key, own, number, rows, number_of, top, most, skew):
    sequence = jax.random.permutation(stream_key, number_of)
    crowded, usual = shares(number_of, rows * top, most, skew, True), shares(number_of, rows * top, most, skew, False)
    places = jnp.arange(number_of)

    def named(lengths, turn):
        used = int((lengths > 0).sum())
        fixed = max(1, used // 4)
        moved = fixed + (places - fixed + turn * (used - fixed)) % max(1, number_of - fixed)
        return jnp.zeros((number_of,), jnp.int32).at[sequence[jnp.where(places < fixed, places, moved)]].set(jnp.asarray(lengths, jnp.int32))

    lengths = jnp.where(number % 4 == 0, named(crowded, number // 4), named(usual, number - number // 4 - 1))
    mixed = jax.random.permutation(jax.random.fold_in(own, 3), number_of)
    giver, taker = mixed[0:number_of // 2 * 2:2], mixed[1:number_of // 2 * 2:2]
    slack = jnp.minimum(lengths[giver] - 1, most - lengths[taker]) // 2
    slack = jnp.where((giver == sequence[0]) | (taker == sequence[0]) | (lengths[taker] == 0), 0, jnp.maximum(slack, 0))
    moved = jax.random.randint(jax.random.fold_in(own, 4), (number_of // 2,), 0, 1 << 20) % (slack + 1)
    lengths = lengths.at[giver].add(-moved).at[taker].add(moved)
    members = jnp.searchsorted(jnp.cumsum(lengths), jnp.arange(rows * top), side="right").astype(jnp.int32)
    grid = members.reshape(top, rows).T
    grid = grid[jax.random.permutation(jax.random.fold_in(own, 1), rows)]
    turn = jax.random.randint(jax.random.fold_in(own, 2), (rows, 1), 0, top)
    return jnp.take_along_axis(grid, (jnp.arange(top)[None, :] + turn) % top, axis=1)


def shares(amount, total, most, lean, full):
    loads = [(1 << 20) // math.isqrt(standing ** lean) + 1 for standing in range(1, amount + 1)]
    largest = most if full else min(most, max(-(-total // amount), total * loads[0] // sum(loads)))
    least = 1 if total - largest >= amount - 1 else 0
    counts, surplus = [largest] + [least] * (amount - 1), total - largest - least * (amount - 1)
    while surplus > 0:
        movable = [i for i in range(1, amount) if counts[i] < largest] or [i for i in range(1, amount) if counts[i] < most]
        pool, budget = sum([loads[i] for i in movable]), surplus
        for i in movable:
            extra = min(most - counts[i], max(1, budget * loads[i] // pool), surplus)
            counts[i] = counts[i] + extra
            surplus = surplus - extra
    return np.array(counts)


def bell_draw(rng, extent, width, most, split=(), kind=jnp.bfloat16):
    factor_of = shard_levels(rng, extent, split, -0.22, 0.18) if split else 1.0
    values = jax.random.normal(rng, extent, jnp.float32) * width * factor_of
    return jnp.minimum(jnp.maximum(values, -most), most).astype(kind)


def setup_inputs(seed: int = 0, part: int = 0) -> dict:
    arg_keys = jax.random.split(jax.random.key(seed), 8)
    part_splits = jax.random.split(jax.random.fold_in(arg_keys[7], part), 8)
    activations = bell_draw(part_splits[0], (TOKENS, D), 1.0, 6.0, ((0, 4), (1, 4)))
    out_grad = bell_draw(part_splits[1], (TOKENS, D), 1.0, 6.0, ((0, 4), (1, 4)))
    routes_keys = jax.random.split(jax.random.fold_in(part_splits[2], 1), TOKENS // TOK_DEV)
    routes_turns = jax.random.permutation(jax.random.fold_in(part_splits[2], 3), TOKENS // TOK_DEV)
    routes = jax.vmap(lambda own, number: shared_out(jax.random.fold_in(part_splits[2], 2), own, number, TOK_DEV, EXPERTS, TOP, CAP, 2))(routes_keys, routes_turns).reshape((TOKENS, TOP))
    gates = jnp.clip(jnp.exp(math.log(1.0) - 2.3025851 * jax.random.uniform(part_splits[3], (TOKENS, TOP), jnp.float32) ** shard_levels(part_splits[3], (TOKENS, TOP), ((0, 4),), -0.2, 0.2)), 0.1, 1.0)
    gate_weight = bell_draw(arg_keys[4], (EXPERTS, D, FF), D ** -0.5, 0.0625, ((0, 4), (2, 4)))
    up_weight = bell_draw(arg_keys[5], (EXPERTS, D, FF), D ** -0.5, 0.0625, ((0, 4), (2, 4)))
    down_weight = bell_draw(arg_keys[6], (EXPERTS, FF, D), FF ** -0.5, 0.125, ((0, 4), (1, 4)))
    return dict(activations=activations, out_grad=out_grad, routes=routes, gates=gates, gate_weight=gate_weight, up_weight=up_weight, down_weight=down_weight)


def expert_grads(x_rows, d_rows, w_gate, w_up, w_down):
    pre_gate = jnp.dot(x_rows, w_gate, preferred_element_type=jnp.float32)
    pre_up = jnp.dot(x_rows, w_up, preferred_element_type=jnp.float32)
    hidden_grad = lax.dot_general(d_rows, w_down, (((1,), (1,)), ((), ())), preferred_element_type=jnp.float32)
    sigma = jax.nn.sigmoid(pre_gate)
    gate_grad = (hidden_grad * pre_up * sigma * (1.0 + pre_gate * (1.0 - sigma))).astype(jnp.bfloat16)
    up_grad = (hidden_grad * pre_gate * sigma).astype(jnp.bfloat16)
    first = lax.dot_general(gate_grad, w_gate, (((1,), (1,)), ((), ())), preferred_element_type=jnp.float32)
    second = lax.dot_general(up_grad, w_up, (((1,), (1,)), ((), ())), preferred_element_type=jnp.float32)
    return first + second


def reference(activations, out_grad, routes, gates, gate_weight, up_weight, down_weight):
    pair_count = TOKENS * TOP
    flat_ids = routes.reshape(-1).astype(jnp.int32)
    flat_gates = gates.reshape(-1)
    base_index = jnp.arange(pair_count, dtype=jnp.int32)
    slot_total = EXPERTS * CAP
    block_width = FF // N_TENSOR

    def per_expert(carry, inputs):
        expert_id, w_gate, w_up, w_down = inputs
        sort_keys = jnp.where(flat_ids == expert_id, base_index, base_index + pair_count)
        picked = jnp.argsort(sort_keys)[:slot_total].astype(jnp.int32)
        filled = flat_ids[picked] == expert_id
        row_index = picked // TOP
        x_slots = jnp.where(filled[:, None], activations[row_index], jnp.zeros((), activations.dtype))
        slot_gate = jnp.where(filled, flat_gates[picked], jnp.zeros((), flat_gates.dtype))
        d_slots = (slot_gate[:, None] * out_grad[row_index].astype(jnp.float32)).astype(jnp.bfloat16)
        running = jnp.zeros((slot_total, D), jnp.float32)
        for block_index in range(N_TENSOR):
            lower = block_index * block_width
            upper = lower + block_width
            partial_value = expert_grads(x_slots, d_slots, w_gate[:, lower:upper], w_up[:, lower:upper], w_down[lower:upper, :])
            rounded = lax.optimization_barrier(partial_value.astype(jnp.bfloat16))
            running = running + rounded.astype(jnp.float32)
        slot_grad = lax.optimization_barrier(running.astype(jnp.bfloat16)).astype(jnp.float32)
        slot_grad = jnp.where(filled[:, None], slot_grad, jnp.zeros((), jnp.float32))
        return carry.at[row_index].add(slot_grad), None

    start = jnp.zeros((TOKENS, D), jnp.float32)
    expert_ids = jnp.arange(EXPERTS, dtype=jnp.int32)
    summed, unused = lax.scan(per_expert, start, (expert_ids, gate_weight, up_weight, down_weight))
    return summed.astype(jnp.bfloat16)
```

```python
import functools

import jax
import jax.numpy as jnp
from jax import lax
from jax.experimental import pallas as pl
from jax.experimental.pallas import tpu as pltpu
from jax.sharding import PartitionSpec as P

MESH = pl.DeviceIdType.MESH
F32 = jnp.float32
BF16 = jnp.bfloat16
NT = (((1,), (1,)), ((), ()))


def flip(a, k, n):
    out, bit = 0, 1
    while bit < n:
        out = out + bit * lax.rem(lax.div(a, bit) + lax.div(k, bit), 2)
        bit *= 2
    return out


def kernel(
    E, T, cap,
    x_ref, d_ref, routes_ref, gates_ref, wg_hbm, wu_hbm, wd_hbm, out_ref,
    wg, wu, wd, xd_send, xd, pt, pre_g, pre_u, hid, gg, ug, own,
    a_send, a_recv, b_send, b_recv, c_send, c_recv,
    w_sem, zs, zr, xs, xr, cs, cr, as_, ar, bs, br, rs, rr,
):
    X = T // 2
    W = x_ref.shape[1]
    tok = x_ref.shape[0]
    me = lax.axis_index("expert")
    mt = lax.axis_index("tensor")
    mx, mc = lax.div(mt, 2), lax.rem(mt, 2)
    oc = 1 - mc
    partner = mx * 2 + oc

    loads = [
        pltpu.make_async_copy(h, v, w_sem.at[i])
        for i, (h, v) in enumerate(((wg_hbm, wg), (wu_hbm, wu), (wd_hbm, wd)))
    ]
    for c in loads:
        c.start()

    barrier = pltpu.get_barrier_semaphore()

    def greet_z(k, _):
        pl.semaphore_signal(barrier, inc=1, device_id={"expert": lax.rem(me + k, E)}, device_id_type=MESH)
        return 0

    lax.fori_loop(1, E, greet_z, 0)
    for j in range(1, X):
        pl.semaphore_signal(
            barrier, inc=1, device_id={"tensor": lax.rem(mx + j, X) * 2 + mc}, device_id_type=MESH
        )
    pl.semaphore_signal(barrier, inc=1, device_id={"tensor": partner}, device_id_type=MESH)

    lanes = pt.shape[2]
    expert_lane = lax.broadcasted_iota(jnp.int32, (tok, 128), 1)
    first, second = routes_ref[:, 0:1], routes_ref[:, 1:2]
    on_first, on_second = first == expert_lane, second == expert_lane
    named = jnp.where(on_first | on_second, 1.0, 0.0).astype(F32)
    weight = jnp.where(on_first, gates_ref[:, 0:1], 0.0) + jnp.where(on_second, gates_ref[:, 1:2], 0.0)
    row = lax.broadcasted_iota(jnp.int32, (tok, tok), 0)
    col = lax.broadcasted_iota(jnp.int32, (tok, tok), 1)
    before = jnp.where(col < row, 1.0, 0.0).astype(BF16)
    rank = jnp.dot(before, named.astype(BF16), preferred_element_type=F32)
    place = jnp.where(named > 0, rank, -1.0)
    slot_lane = lax.broadcasted_iota(jnp.int32, (tok, lanes), 1).astype(F32)

    def z_copy(e):
        return pltpu.make_async_remote_copy(
            src_ref=xd_send.at[e], dst_ref=xd.at[mt, me], send_sem=zs.at[e], recv_sem=zr.at[me],
            device_id={"expert": e}, device_id_type=MESH,
        )

    def z_arrival(s):
        return pltpu.make_async_remote_copy(
            src_ref=xd_send.at[s], dst_ref=xd.at[mt, s], send_sem=zs.at[s], recv_sem=zr.at[s],
            device_id={"expert": s}, device_id_type=MESH,
        )

    def fill(e, dst):
        chosen = expert_lane == e
        at = jnp.sum(jnp.where(chosen, place, 0.0), axis=1, keepdims=True)
        g = jnp.sum(jnp.where(chosen, weight, 0.0), axis=1, keepdims=True)
        sel = jnp.where(at == slot_lane, 1.0, 0.0).astype(F32)
        pt[e] = sel.astype(BF16)
        sel_t = sel.T[:cap]
        slot_gate = jnp.sum((sel * g).T[:cap], axis=1, keepdims=True)
        pick = sel_t.astype(BF16)
        dst[0:cap, :] = jnp.dot(pick, x_ref[...], preferred_element_type=F32).astype(BF16)
        d_rows = jnp.dot(pick, d_ref[...], preferred_element_type=F32)
        dst[cap : 2 * cap, :] = (slot_gate * d_rows).astype(BF16)

    def x_copy(s, j):
        return pltpu.make_async_remote_copy(
            src_ref=xd.at[mt, s], dst_ref=xd.at[mt, s],
            send_sem=xs.at[j, s], recv_sem=xr.at[j, s],
            device_id={"tensor": lax.rem(mx + j, X) * 2 + mc}, device_id_type=MESH,
        )

    def x_arrival(s, j):
        src = lax.rem(mx - j + X, X) * 2 + mc
        return pltpu.make_async_remote_copy(
            src_ref=xd.at[src, s], dst_ref=xd.at[src, s],
            send_sem=xs.at[j, s], recv_sem=xr.at[j, s],
            device_id={"tensor": src}, device_id_type=MESH,
        )

    def core_copy(s, xi):
        t = xi * 2 + mc
        return pltpu.make_async_remote_copy(
            src_ref=xd.at[t, s], dst_ref=xd.at[t, s], send_sem=cs.at[xi, s], recv_sem=cr.at[xi, s],
            device_id={"tensor": partner}, device_id_type=MESH,
        )

    def core_arrival(s, xi):
        t = xi * 2 + oc
        return pltpu.make_async_remote_copy(
            src_ref=xd.at[t, s], dst_ref=xd.at[t, s], send_sem=cs.at[xi, s], recv_sem=cr.at[xi, s],
            device_id={"tensor": partner}, device_id_type=MESH,
        )

    def spread(s):
        for j in range(1, X):
            x_copy(s, j).start()
        core_copy(s, mx).start()

    def a_copy(s, xi):
        return pltpu.make_async_remote_copy(
            src_ref=a_send.at[s, xi], dst_ref=a_recv.at[s, xi],
            send_sem=as_.at[xi, s], recv_sem=ar.at[xi, s],
            device_id={"tensor": partner}, device_id_type=MESH,
        )

    def b_copy(s, j):
        return pltpu.make_async_remote_copy(
            src_ref=b_send.at[s, j], dst_ref=b_recv.at[s, j],
            send_sem=bs.at[j, s], recv_sem=br.at[j, s],
            device_id={"tensor": lax.rem(mx + j, X) * 2 + mc}, device_id_type=MESH,
        )

    def c_copy(s):
        return pltpu.make_async_remote_copy(
            src_ref=c_send.at[s], dst_ref=c_recv.at[me], send_sem=rs.at[s], recv_sem=rr.at[me],
            device_id={"expert": s}, device_id_type=MESH,
        )

    def c_arrival(s):
        return pltpu.make_async_remote_copy(
            src_ref=c_send.at[s], dst_ref=c_recv.at[s], send_sem=rs.at[s], recv_sem=rr.at[s],
            device_id={"expert": s}, device_id_type=MESH,
        )

    fill(me, xd.at[mt, me])
    pl.semaphore_wait(barrier, (E - 1) + (X - 1) + 1)
    spread(me)

    def send_z(k, _):
        e = flip(me, k, E)
        fill(e, xd_send.at[e])
        z_copy(e).start()
        return 0

    lax.fori_loop(1, E, send_z, 0)
    for c in loads:
        c.wait()

    def forward(s, t):
        wide = pl.ds(pl.multiple_of(t * W, W), W)
        x_rows = xd[t, s, 0:cap, :]
        d_rows = xd[t, s, cap : 2 * cap, :]
        pre_g[...] += jnp.dot(x_rows, wg[wide, :], preferred_element_type=F32)
        pre_u[...] += jnp.dot(x_rows, wu[wide, :], preferred_element_type=F32)
        hid[...] += lax.dot_general(d_rows, wd[:, wide], NT, preferred_element_type=F32)

    def part_of(t):
        wide = pl.ds(pl.multiple_of(t * W, W), W)
        return lax.dot_general(gg[...], wg[wide, :], NT, preferred_element_type=F32) + lax.dot_general(
            ug[...], wu[wide, :], NT, preferred_element_type=F32
        )

    def finish(s):
        total = own[s]
        for j in range(1, X):
            b_copy(s, j).wait_recv()
            total = total + b_recv[s, j].astype(F32)
        c_send[s] = total.astype(BF16)

        @pl.when(s != me)
        def _():
            c_copy(s).start()

    def chunk(k, _):
        s = flip(me, k, E)

        @pl.when(k + 1 < E)
        def _():
            ahead = flip(me, k + 1, E)
            z_arrival(ahead).wait_recv()
            spread(ahead)

        pre_g[...] = jnp.zeros_like(pre_g)
        pre_u[...] = jnp.zeros_like(pre_u)
        hid[...] = jnp.zeros_like(hid)

        def slice_step(i, _):
            @pl.when(i == 1)
            def _():
                core_arrival(s, mx).wait_recv()

            for j in range(1, X):
                src = lax.rem(mx - j + X, X)

                @pl.when(i == 1 + j)
                def _():
                    x_arrival(s, j).wait_recv()
                    core_copy(s, src).start()

                @pl.when(i == X + j)
                def _():
                    core_arrival(s, src).wait_recv()

            j = jnp.where(i < 2, 0, jnp.where(i <= X, i - 1, i - X))
            other = jnp.where(i < 2, i, jnp.where(i <= X, 0, 1))
            xi = lax.rem(mx - j + X, X)
            core = lax.rem(mc + other, 2)
            forward(s, xi * 2 + core)
            return 0

        lax.fori_loop(0, T, slice_step, 0)

        pg, pu, hg = pre_g[...], pre_u[...], hid[...]
        sigma = jax.nn.sigmoid(pg)
        gg[...] = (hg * pu * sigma * (1.0 + pg * (1.0 - sigma))).astype(BF16)
        ug[...] = (hg * pg * sigma).astype(BF16)

        def give(i, _):
            xi = lax.rem(mx + 1 + i, X)
            a_send[s, xi] = part_of(xi * 2 + oc).astype(BF16)
            a_copy(s, xi).start()
            return 0

        lax.fori_loop(0, X, give, 0)

        def keep(j, _):
            xi = lax.rem(mx + j, X)
            mine = part_of(xi * 2 + mc)
            a_copy(s, xi).wait_recv()
            b_send[s, j] = (mine + a_recv[s, xi].astype(F32)).astype(BF16)
            b_copy(s, j).start()
            return 0

        lax.fori_loop(1, X, keep, 0)
        mine = part_of(mx * 2 + mc)
        a_copy(s, mx).wait_recv()
        own[s] = mine + a_recv[s, mx].astype(F32)

        @pl.when(k >= 1)
        def _():
            finish(flip(me, k - 1, E))

        return 0

    lax.fori_loop(0, E, chunk, 0)
    finish(flip(me, E - 1, E))

    def add(s, _):
        @pl.when(s != me)
        def _():
            c_arrival(s).wait_recv()

        return 0

    lax.fori_loop(0, E, add, 0)
    total = jnp.dot(pt[me, :, :cap], c_send[me], preferred_element_type=F32)
    for k in range(1, E):
        s = flip(me, k, E)
        total = total + jnp.dot(pt[s, :, :cap], c_recv[s], preferred_element_type=F32)
    out_ref[...] = total.astype(BF16)

    def drain(s, _):
        @pl.when(s != me)
        def _():
            z_copy(s).wait_send()
            c_copy(s).wait_send()

        for j in range(1, X):
            x_copy(s, j).wait_send()
            b_copy(s, j).wait_send()
        for xi in range(X):
            core_copy(s, xi).wait_send()
            a_copy(s, xi).wait_send()
        return 0

    lax.fori_loop(0, E, drain, 0)


def per_device(activations, out_grad, routes, gates, gate_weight, up_weight, down_weight):
    E = lax.axis_size("expert")
    T = lax.axis_size("tensor")
    X = T // 2
    tok, top = routes.shape
    W = activations.shape[1]
    D, FF = gate_weight.shape[1:]
    need = 3 * tok * top // (2 * E)
    cap = -(-need // 16) * 16
    wide = -(-cap // 128) * 128
    vmem = pl.BlockSpec(memory_space=pltpu.VMEM)
    anywhere = pl.BlockSpec(memory_space=pl.ANY)
    dma = pltpu.SemaphoreType.DMA
    return pl.pallas_call(
        functools.partial(kernel, E, T, cap),
        out_shape=jax.ShapeDtypeStruct((tok, W), BF16),
        in_specs=[vmem] * 4 + [anywhere] * 3,
        out_specs=vmem,
        scratch_shapes=[
            pltpu.VMEM((D, FF), BF16),
            pltpu.VMEM((D, FF), BF16),
            pltpu.VMEM((FF, D), BF16),
            pltpu.VMEM((E, 2 * cap, W), BF16),
            pltpu.VMEM((T, E, 2 * cap, W), BF16),
            pltpu.VMEM((E, tok, wide), BF16),
            pltpu.VMEM((cap, FF), F32),
            pltpu.VMEM((cap, FF), F32),
            pltpu.VMEM((cap, FF), F32),
            pltpu.VMEM((cap, FF), BF16),
            pltpu.VMEM((cap, FF), BF16),
            pltpu.VMEM((E, cap, W), F32),
            pltpu.VMEM((E, X, cap, W), BF16),
            pltpu.VMEM((E, X, cap, W), BF16),
            pltpu.VMEM((E, X, cap, W), BF16),
            pltpu.VMEM((E, X, cap, W), BF16),
            pltpu.VMEM((E, cap, W), BF16),
            pltpu.VMEM((E, cap, W), BF16),
            dma((3,)),
            dma((E,)), dma((E,)),
            dma((X, E)), dma((X, E)),
            dma((X, E)), dma((X, E)),
            dma((X, E)), dma((X, E)),
            dma((X, E)), dma((X, E)),
            dma((E,)), dma((E,)),
        ],
        compiler_params=pltpu.CompilerParams(
            collective_id=0, has_side_effects=True, vmem_limit_bytes=62 * 1024 * 1024
        ),
        cost_estimate=pl.CostEstimate(
            flops=10 * E * cap * D * FF, bytes_accessed=6 * D * FF, transcendentals=E * cap * FF
        ),
    )(activations, out_grad, routes, gates, gate_weight[0], up_weight[0], down_weight[0])


def solution(mesh):
    return jax.shard_map(
        per_device,
        mesh=mesh,
        in_specs=(
            P(("group", "expert"), "tensor"),
            P(("group", "expert"), "tensor"),
            P(("group", "expert"), None),
            P(("group", "expert"), None),
            P("expert", None, "tensor"),
            P("expert", None, "tensor"),
            P("expert", "tensor", None),
        ),
        out_specs=P(("group", "expert"), "tensor"),
        check_vma=False,
    )
```

```python
import functools

import jax
import jax.numpy as jnp
from jax import lax
from jax.experimental import pallas as pl
from jax.experimental.pallas import tpu as pltpu
from jax.sharding import PartitionSpec as P

MESH = pl.DeviceIdType.MESH
F32 = jnp.float32
BF16 = jnp.bfloat16
NT = (((1,), (1,)), ((), ()))
TN = (((0,), (0,)), ((), ()))


def nth(z, k, n):
    low = z < n // 2
    edge = jnp.where(low, z, n - 1 - z)
    step = jnp.where(low, -1, 1)
    odd = lax.rem(k, 2)
    near = jnp.where(odd == 1, step * lax.div(k + 1, 2), -step * lax.div(k, 2))
    return z + jnp.where(k <= 2 * edge, near, -step * (k - edge))


def kernel(
    E, T, cap,
    x_ref, d_ref, routes_ref, gates_ref, wg_hbm, wu_hbm, wd_hbm, out_ref,
    wg, wu, wd, xd_send, xd, pt, pre_g, pre_u, hid, gg, ug, own,
    a_send, a_recv, b_send, b_recv, c_send, c_recv,
    w_sem, zs, zr, xs, xr, cs, cr, as_, ar, bs, br, rs, rr,
):
    X = T // 2
    W = x_ref.shape[1]
    tok = x_ref.shape[0]
    me = lax.axis_index("expert")
    mt = lax.axis_index("tensor")
    mx, mc = lax.div(mt, 2), lax.rem(mt, 2)
    oc = 1 - mc
    partner = mx * 2 + oc

    loads = [
        pltpu.make_async_copy(h, v, w_sem.at[i])
        for i, (h, v) in enumerate(((wg_hbm, wg), (wu_hbm, wu), (wd_hbm, wd)))
    ]
    for c in loads:
        c.start()

    barrier = pltpu.get_barrier_semaphore()

    def greet_z(k, _):
        pl.semaphore_signal(barrier, inc=1, device_id={"expert": lax.rem(me + k, E)}, device_id_type=MESH)
        return 0

    lax.fori_loop(1, E, greet_z, 0)
    for j in range(1, X):
        pl.semaphore_signal(
            barrier, inc=1, device_id={"tensor": lax.rem(mx + j, X) * 2 + mc}, device_id_type=MESH
        )
    pl.semaphore_signal(barrier, inc=1, device_id={"tensor": partner}, device_id_type=MESH)

    deep = -(-E // 16) * 16
    expert_row = lax.broadcasted_iota(jnp.int32, (deep, tok), 0)
    on_first, on_second = routes_ref[0:1, :] == expert_row, routes_ref[1:2, :] == expert_row
    named = jnp.where(on_first | on_second, 1.0, 0.0).astype(F32)
    weight = jnp.where(on_first, gates_ref[0:1, :], 0.0) + jnp.where(on_second, gates_ref[1:2, :], 0.0)
    row = lax.broadcasted_iota(jnp.int32, (tok, tok), 0)
    col = lax.broadcasted_iota(jnp.int32, (tok, tok), 1)
    earlier = jnp.where(row < col, 1.0, 0.0).astype(BF16)
    rank = jnp.dot(named.astype(BF16), earlier, preferred_element_type=F32)
    place = jnp.where(named > 0, rank, -1.0)
    slot_row = lax.broadcasted_iota(jnp.int32, (cap, tok), 0).astype(F32)

    def z_copy(e, h):
        return pltpu.make_async_remote_copy(
            src_ref=xd_send.at[e, h], dst_ref=xd.at[mt, me, h], send_sem=zs.at[h, e], recv_sem=zr.at[h, me],
            device_id={"expert": e}, device_id_type=MESH,
        )

    def z_arrival(s, h):
        return pltpu.make_async_remote_copy(
            src_ref=xd_send.at[s, h], dst_ref=xd.at[mt, s, h], send_sem=zs.at[h, s], recv_sem=zr.at[h, s],
            device_id={"expert": s}, device_id_type=MESH,
        )

    def fill(e, dst):
        chosen = expert_row == e
        at = jnp.sum(jnp.where(chosen, place, 0.0), axis=0, keepdims=True)
        g = jnp.sum(jnp.where(chosen, weight, 0.0), axis=0, keepdims=True)
        sel = jnp.where(at == slot_row, 1.0, 0.0).astype(F32)
        slot_gate = jnp.sum(sel * g, axis=1, keepdims=True)
        pick = sel.astype(BF16)
        pt[e] = pick
        dst[0] = jnp.dot(pick, x_ref[...], preferred_element_type=F32).astype(BF16)
        d_rows = jnp.dot(pick, d_ref[...], preferred_element_type=F32)
        dst[1] = (slot_gate * d_rows).astype(BF16)

    def x_copy(s, h, j):
        return pltpu.make_async_remote_copy(
            src_ref=xd.at[mt, s, h], dst_ref=xd.at[mt, s, h],
            send_sem=xs.at[h, j, s], recv_sem=xr.at[h, j, s],
            device_id={"tensor": lax.rem(mx + j, X) * 2 + mc}, device_id_type=MESH,
        )

    def x_arrival(s, h, j):
        src = lax.rem(mx - j + X, X) * 2 + mc
        return pltpu.make_async_remote_copy(
            src_ref=xd.at[src, s, h], dst_ref=xd.at[src, s, h],
            send_sem=xs.at[h, j, s], recv_sem=xr.at[h, j, s],
            device_id={"tensor": src}, device_id_type=MESH,
        )

    def core_copy(s, h, xi):
        t = xi * 2 + mc
        return pltpu.make_async_remote_copy(
            src_ref=xd.at[t, s, h], dst_ref=xd.at[t, s, h],
            send_sem=cs.at[h, xi, s], recv_sem=cr.at[h, xi, s],
            device_id={"tensor": partner}, device_id_type=MESH,
        )

    def core_arrival(s, h, xi):
        t = xi * 2 + oc
        return pltpu.make_async_remote_copy(
            src_ref=xd.at[t, s, h], dst_ref=xd.at[t, s, h],
            send_sem=cs.at[h, xi, s], recv_sem=cr.at[h, xi, s],
            device_id={"tensor": partner}, device_id_type=MESH,
        )

    def spread(s, h):
        for j in range(1, X):
            x_copy(s, h, j).start()
        core_copy(s, h, mx).start()

    def a_copy(s, xi):
        return pltpu.make_async_remote_copy(
            src_ref=a_send.at[s, xi], dst_ref=a_recv.at[s, xi],
            send_sem=as_.at[xi, s], recv_sem=ar.at[xi, s],
            device_id={"tensor": partner}, device_id_type=MESH,
        )

    half = cap // 2

    def b_copy(s, j, h):
        rows = pl.ds(h * half, half)
        return pltpu.make_async_remote_copy(
            src_ref=b_send.at[s, j, rows], dst_ref=b_recv.at[s, j, rows],
            send_sem=bs.at[h, j, s], recv_sem=br.at[h, j, s],
            device_id={"tensor": lax.rem(mx + j, X) * 2 + mc}, device_id_type=MESH,
        )

    def c_copy(s, h):
        rows = pl.ds(h * half, half)
        return pltpu.make_async_remote_copy(
            src_ref=c_send.at[s, rows], dst_ref=c_recv.at[me, rows],
            send_sem=rs.at[h, s], recv_sem=rr.at[h, me],
            device_id={"expert": s}, device_id_type=MESH,
        )

    def c_arrival(s, h):
        rows = pl.ds(h * half, half)
        return pltpu.make_async_remote_copy(
            src_ref=c_send.at[s, rows], dst_ref=c_recv.at[s, rows],
            send_sem=rs.at[h, s], recv_sem=rr.at[h, s],
            device_id={"expert": s}, device_id_type=MESH,
        )

    fill(me, xd.at[mt, me])
    pl.semaphore_wait(barrier, (E - 1) + (X - 1) + 1)
    for h in range(2):
        spread(me, h)

    ahead_of = jnp.where((me == 0) | (me == E - 1), 1, 2)

    def send_z(k, _):
        e = nth(me, k, E)
        fill(e, xd_send.at[e])

        @pl.when(k <= ahead_of)
        def _():
            for h in range(2):
                z_copy(e, h).start()

        return 0

    lax.fori_loop(1, E, send_z, 0)
    for c in loads:
        c.wait()

    def forward(s, h, t):
        wide = pl.ds(pl.multiple_of(t * W, W), W)
        rows = xd[t, s, h]
        if h == 0:
            pre_g[...] += jnp.dot(rows, wg[wide, :], preferred_element_type=F32)
            pre_u[...] += jnp.dot(rows, wu[wide, :], preferred_element_type=F32)
        else:
            hid[...] += lax.dot_general(rows, wd[:, wide], NT, preferred_element_type=F32)

    def part_of(t):
        wide = pl.ds(pl.multiple_of(t * W, W), W)
        return lax.dot_general(gg[...], wg[wide, :], NT, preferred_element_type=F32) + lax.dot_general(
            ug[...], wu[wide, :], NT, preferred_element_type=F32
        )

    def finish(s):
        for h in range(2):
            rows = pl.ds(h * half, half)
            total = own[s, rows]
            for j in range(1, X):
                b_copy(s, j, h).wait_recv()
                total = total + b_recv[s, j, rows].astype(F32)
            c_send[s, rows] = total.astype(BF16)

            @pl.when(s != me)
            def _():
                c_copy(s, h).start()

    def arrive(k, h):
        @pl.when(k < E)
        def _():
            s = nth(me, k, E)
            z_arrival(s, h).wait_recv()
            spread(s, h)

        @pl.when((k >= ahead_of) & (k + 1 < E))
        def _():
            z_copy(nth(me, k + 1, E), h).start()

    def chunk(k, _):
        s = nth(me, k, E)
        arrive(k + 1, 0)

        pre_g[...] = jnp.zeros_like(pre_g)
        pre_u[...] = jnp.zeros_like(pre_u)
        hid[...] = jnp.zeros_like(hid)

        def slice_step(h, i, _):
            @pl.when(i == 1)
            def _():
                core_arrival(s, h, mx).wait_recv()

            for j in range(1, X):
                src = lax.rem(mx - j + X, X)

                @pl.when(i == 1 + j)
                def _():
                    x_arrival(s, h, j).wait_recv()
                    core_copy(s, h, src).start()

                @pl.when(i == X + j)
                def _():
                    core_arrival(s, h, src).wait_recv()

            j = jnp.where(i < 2, 0, jnp.where(i <= X, i - 1, i - X))
            other = jnp.where(i < 2, i, jnp.where(i <= X, 0, 1))
            xi = lax.rem(mx - j + X, X)
            core = lax.rem(mc + other, 2)
            forward(s, h, xi * 2 + core)
            return 0

        lax.fori_loop(0, T, functools.partial(slice_step, 0), 0)

        @pl.when(k == 0)
        def _():
            arrive(1, 1)

        lax.fori_loop(0, T, functools.partial(slice_step, 1), 0)

        @pl.when(k == E - 2)
        def _():
            arrive(k + 1, 1)

        pg, pu, hg = pre_g[...], pre_u[...], hid[...]
        sigma = jax.nn.sigmoid(pg)
        gg[...] = (hg * pu * sigma * (1.0 + pg * (1.0 - sigma))).astype(BF16)
        ug[...] = (hg * pg * sigma).astype(BF16)

        def give(xi):
            a_send[s, xi] = part_of(xi * 2 + oc).astype(BF16)
            a_copy(s, xi).start()
            mine = part_of(xi * 2 + mc)
            a_copy(s, xi).wait_recv()
            return mine + a_recv[s, xi].astype(F32)

        def keep(j, _):
            b_send[s, j] = give(lax.rem(mx + j, X)).astype(BF16)
            for h in range(2):
                b_copy(s, j, h).start()
            return 0

        lax.fori_loop(1, X, keep, 0)
        @pl.when(k >= 1)
        def _():
            finish(nth(me, k - 1, E))

        own[s] = give(mx)

        @pl.when((k > 0) & (k < E - 2))
        def _():
            arrive(k + 1, 1)


        return 0

    lax.fori_loop(0, E, chunk, 0)
    finish(nth(me, E - 1, E))

    total = lax.dot_general(pt[me], c_send[me], TN, preferred_element_type=F32)
    for k in range(1, E):
        s = nth(me, k, E)
        for h in range(2):
            c_arrival(s, h).wait_recv()
        total = total + lax.dot_general(pt[s], c_recv[s], TN, preferred_element_type=F32)
    out_ref[...] = total.astype(BF16)

    def drain(s, _):
        for h in range(2):

            @pl.when(s != me)
            def _():
                z_copy(s, h).wait_send()
                c_copy(s, h).wait_send()

            for j in range(1, X):
                x_copy(s, h, j).wait_send()
                b_copy(s, j, h).wait_send()
            for xi in range(X):
                core_copy(s, h, xi).wait_send()
        for xi in range(X):
            a_copy(s, xi).wait_send()
        return 0

    lax.fori_loop(0, E, drain, 0)


def per_device(activations, out_grad, routes, gates, gate_weight, up_weight, down_weight):
    E = lax.axis_size("expert")
    T = lax.axis_size("tensor")
    X = T // 2
    tok, top = routes.shape
    W = activations.shape[1]
    D, FF = gate_weight.shape[1:]
    need = 3 * tok * top // (2 * E)
    cap = -(-need // 32) * 32
    vmem = pl.BlockSpec(memory_space=pltpu.VMEM)
    anywhere = pl.BlockSpec(memory_space=pl.ANY)
    dma = pltpu.SemaphoreType.DMA
    return pl.pallas_call(
        functools.partial(kernel, E, T, cap),
        out_shape=jax.ShapeDtypeStruct((tok, W), BF16),
        in_specs=[vmem] * 4 + [anywhere] * 3,
        out_specs=vmem,
        scratch_shapes=[
            pltpu.VMEM((D, FF), BF16),
            pltpu.VMEM((D, FF), BF16),
            pltpu.VMEM((FF, D), BF16),
            pltpu.VMEM((E, 2, cap, W), BF16),
            pltpu.VMEM((T, E, 2, cap, W), BF16),
            pltpu.VMEM((E, cap, tok), BF16),
            pltpu.VMEM((cap, FF), F32),
            pltpu.VMEM((cap, FF), F32),
            pltpu.VMEM((cap, FF), F32),
            pltpu.VMEM((cap, FF), BF16),
            pltpu.VMEM((cap, FF), BF16),
            pltpu.VMEM((E, cap, W), F32),
            pltpu.VMEM((E, X, cap, W), BF16),
            pltpu.VMEM((E, X, cap, W), BF16),
            pltpu.VMEM((E, X, cap, W), BF16),
            pltpu.VMEM((E, X, cap, W), BF16),
            pltpu.VMEM((E, cap, W), BF16),
            pltpu.VMEM((E, cap, W), BF16),
            dma((3,)),
            dma((2, E)), dma((2, E)),
            dma((2, X, E)), dma((2, X, E)),
            dma((2, X, E)), dma((2, X, E)),
            dma((X, E)), dma((X, E)),
            dma((2, X, E)), dma((2, X, E)),
            dma((2, E)), dma((2, E)),
        ],
        compiler_params=pltpu.CompilerParams(
            collective_id=0, has_side_effects=True, vmem_limit_bytes=62 * 1024 * 1024
        ),
        cost_estimate=pl.CostEstimate(
            flops=10 * E * cap * D * FF, bytes_accessed=6 * D * FF, transcendentals=E * cap * FF
        ),
    )(activations, out_grad, routes.T, gates.T, gate_weight[0], up_weight[0], down_weight[0])


def solution(mesh):
    return jax.shard_map(
        per_device,
        mesh=mesh,
        in_specs=(
            P(("group", "expert"), "tensor"),
            P(("group", "expert"), "tensor"),
            P(("group", "expert"), None),
            P(("group", "expert"), None),
            P("expert", None, "tensor"),
            P("expert", None, "tensor"),
            P("expert", "tensor", None),
        ),
        out_specs=P(("group", "expert"), "tensor"),
        check_vma=False,
    )
```

```python
import functools

import jax
import jax.numpy as jnp
from jax import lax
from jax.experimental import pallas as pl
from jax.experimental.pallas import tpu as pltpu
from jax.sharding import PartitionSpec as P

MESH = pl.DeviceIdType.MESH
F32 = jnp.float32
BF16 = jnp.bfloat16
NT = (((1,), (1,)), ((), ()))
TN = (((0,), (0,)), ((), ()))


def nth(z, k, n):
    low = z < n // 2
    edge = jnp.where(low, z, n - 1 - z)
    step = jnp.where(low, -1, 1)
    odd = lax.rem(k, 2)
    near = jnp.where(odd == 1, step * lax.div(k + 1, 2), -step * lax.div(k, 2))
    return z + jnp.where(k <= 2 * edge, near, -step * (k - edge))


def kernel(
    E, T, cap,
    x_ref, d_ref, routes_ref, gates_ref, wg_hbm, wu_hbm, wd_hbm, out_ref,
    wg, wu, wd, xd_send, xd, pt, pre_g, pre_u, hid, gg, ug, own,
    a_send, a_recv, b_send, b_recv, c_send, c_recv,
    w_sem, zs, zr, xs, xr, cs, cr, as_, ar, bs, br, rs, rr,
):
    X = T // 2
    W = x_ref.shape[1]
    tok = x_ref.shape[0]
    me = lax.axis_index("expert")
    mt = lax.axis_index("tensor")
    mx, mc = lax.div(mt, 2), lax.rem(mt, 2)
    oc = 1 - mc
    partner = mx * 2 + oc

    loads = [
        pltpu.make_async_copy(h, v, w_sem.at[i])
        for i, (h, v) in enumerate(((wg_hbm, wg), (wu_hbm, wu), (wd_hbm, wd)))
    ]
    for c in loads:
        c.start()

    barrier = pltpu.get_barrier_semaphore()

    def greet_z(k, _):
        pl.semaphore_signal(barrier, inc=1, device_id={"expert": lax.rem(me + k, E)}, device_id_type=MESH)
        return 0

    lax.fori_loop(1, E, greet_z, 0)
    for j in range(1, X):
        pl.semaphore_signal(
            barrier, inc=1, device_id={"tensor": lax.rem(mx + j, X) * 2 + mc}, device_id_type=MESH
        )
    pl.semaphore_signal(barrier, inc=1, device_id={"tensor": partner}, device_id_type=MESH)

    deep = -(-E // 16) * 16
    expert_row = lax.broadcasted_iota(jnp.int32, (deep, tok), 0)
    on_first, on_second = routes_ref[0:1, :] == expert_row, routes_ref[1:2, :] == expert_row
    named = jnp.where(on_first | on_second, 1.0, 0.0).astype(F32)
    weight = jnp.where(on_first, gates_ref[0:1, :], 0.0) + jnp.where(on_second, gates_ref[1:2, :], 0.0)
    row = lax.broadcasted_iota(jnp.int32, (tok, tok), 0)
    col = lax.broadcasted_iota(jnp.int32, (tok, tok), 1)
    earlier = jnp.where(row < col, 1.0, 0.0).astype(BF16)
    rank = jnp.dot(named.astype(BF16), earlier, preferred_element_type=F32)
    place = jnp.where(named > 0, rank, -1.0)
    slot_row = lax.broadcasted_iota(jnp.int32, (cap, tok), 0).astype(F32)

    def z_copy(e, h):
        return pltpu.make_async_remote_copy(
            src_ref=xd_send.at[e, h], dst_ref=xd.at[mt, me, h], send_sem=zs.at[h, e], recv_sem=zr.at[h, me],
            device_id={"expert": e}, device_id_type=MESH,
        )

    def z_arrival(s, h):
        return pltpu.make_async_remote_copy(
            src_ref=xd_send.at[s, h], dst_ref=xd.at[mt, s, h], send_sem=zs.at[h, s], recv_sem=zr.at[h, s],
            device_id={"expert": s}, device_id_type=MESH,
        )

    def fill(e, dst):
        chosen = expert_row == e
        at = jnp.sum(jnp.where(chosen, place, 0.0), axis=0, keepdims=True)
        g = jnp.sum(jnp.where(chosen, weight, 0.0), axis=0, keepdims=True)
        sel = jnp.where(at == slot_row, 1.0, 0.0).astype(F32)
        slot_gate = jnp.sum(sel * g, axis=1, keepdims=True)
        pick = sel.astype(BF16)
        pt[e] = pick
        dst[0] = jnp.dot(pick, x_ref[...], preferred_element_type=F32).astype(BF16)
        d_rows = jnp.dot(pick, d_ref[...], preferred_element_type=F32)
        dst[1] = (slot_gate * d_rows).astype(BF16)

    def x_copy(s, h, j):
        return pltpu.make_async_remote_copy(
            src_ref=xd.at[mt, s, h], dst_ref=xd.at[mt, s, h],
            send_sem=xs.at[h, j, s], recv_sem=xr.at[h, j, s],
            device_id={"tensor": lax.rem(mx + j, X) * 2 + mc}, device_id_type=MESH,
        )

    def x_arrival(s, h, j):
        src = lax.rem(mx - j + X, X) * 2 + mc
        return pltpu.make_async_remote_copy(
            src_ref=xd.at[src, s, h], dst_ref=xd.at[src, s, h],
            send_sem=xs.at[h, j, s], recv_sem=xr.at[h, j, s],
            device_id={"tensor": src}, device_id_type=MESH,
        )

    def core_copy(s, h, xi):
        t = xi * 2 + mc
        return pltpu.make_async_remote_copy(
            src_ref=xd.at[t, s, h], dst_ref=xd.at[t, s, h],
            send_sem=cs.at[h, xi, s], recv_sem=cr.at[h, xi, s],
            device_id={"tensor": partner}, device_id_type=MESH,
        )

    def core_arrival(s, h, xi):
        t = xi * 2 + oc
        return pltpu.make_async_remote_copy(
            src_ref=xd.at[t, s, h], dst_ref=xd.at[t, s, h],
            send_sem=cs.at[h, xi, s], recv_sem=cr.at[h, xi, s],
            device_id={"tensor": partner}, device_id_type=MESH,
        )

    def spread(s, h):
        core_copy(s, h, mx).start()
        for j in range(1, X):
            x_copy(s, h, j).start()

    def a_copy(s, xi):
        return pltpu.make_async_remote_copy(
            src_ref=a_send.at[s, xi], dst_ref=a_recv.at[s, xi],
            send_sem=as_.at[xi, s], recv_sem=ar.at[xi, s],
            device_id={"tensor": partner}, device_id_type=MESH,
        )

    half = cap // 2

    def b_copy(s, j, h):
        rows = pl.ds(h * half, half)
        return pltpu.make_async_remote_copy(
            src_ref=b_send.at[s, j, rows], dst_ref=b_recv.at[s, j, rows],
            send_sem=bs.at[h, j, s], recv_sem=br.at[h, j, s],
            device_id={"tensor": lax.rem(mx + j, X) * 2 + mc}, device_id_type=MESH,
        )

    def c_copy(s, h):
        rows = pl.ds(h * half, half)
        return pltpu.make_async_remote_copy(
            src_ref=c_send.at[s, rows], dst_ref=c_recv.at[me, rows],
            send_sem=rs.at[h, s], recv_sem=rr.at[h, me],
            device_id={"expert": s}, device_id_type=MESH,
        )

    def c_arrival(s, h):
        rows = pl.ds(h * half, half)
        return pltpu.make_async_remote_copy(
            src_ref=c_send.at[s, rows], dst_ref=c_recv.at[s, rows],
            send_sem=rs.at[h, s], recv_sem=rr.at[h, s],
            device_id={"expert": s}, device_id_type=MESH,
        )

    fill(me, xd.at[mt, me])
    pl.semaphore_wait(barrier, (E - 1) + (X - 1) + 1)
    for h in range(2):
        spread(me, h)

    ahead_of = jnp.where((me == 0) | (me == E - 1), 1, 2)

    def send_z(k, _):
        e = nth(me, k, E)
        fill(e, xd_send.at[e])

        @pl.when(k <= ahead_of)
        def _():
            for h in range(2):
                z_copy(e, h).start()

        return 0

    lax.fori_loop(1, E, send_z, 0)
    for c in loads:
        c.wait()

    def forward(s, h, t):
        wide = pl.ds(pl.multiple_of(t * W, W), W)
        rows = xd[t, s, h]
        if h == 0:
            pre_g[...] += jnp.dot(rows, wg[wide, :], preferred_element_type=F32)
            pre_u[...] += jnp.dot(rows, wu[wide, :], preferred_element_type=F32)
        else:
            hid[...] += lax.dot_general(rows, wd[:, wide], NT, preferred_element_type=F32)

    def part_of(t):
        wide = pl.ds(pl.multiple_of(t * W, W), W)
        return lax.dot_general(gg[...], wg[wide, :], NT, preferred_element_type=F32) + lax.dot_general(
            ug[...], wu[wide, :], NT, preferred_element_type=F32
        )

    def finish(s):
        for h in range(2):
            rows = pl.ds(h * half, half)
            total = own[s, rows]
            for j in range(1, X):
                b_copy(s, j, h).wait_recv()
                total = total + b_recv[s, j, rows].astype(F32)
            c_send[s, rows] = total.astype(BF16)

            @pl.when(s != me)
            def _():
                c_copy(s, h).start()

    def arrive(k, h):
        @pl.when(k < E)
        def _():
            s = nth(me, k, E)
            z_arrival(s, h).wait_recv()
            spread(s, h)

        @pl.when((k >= ahead_of) & (k + 1 < E))
        def _():
            z_copy(nth(me, k + 1, E), h).start()

    def chunk(k, _):
        s = nth(me, k, E)
        arrive(k + 1, 0)

        pre_g[...] = jnp.zeros_like(pre_g)
        pre_u[...] = jnp.zeros_like(pre_u)
        hid[...] = jnp.zeros_like(hid)

        def slice_step(h, i, _):
            @pl.when(i == 1)
            def _():
                core_arrival(s, h, mx).wait_recv()

            for j in range(1, X):
                src = lax.rem(mx - j + X, X)

                @pl.when(i == 1 + j)
                def _():
                    x_arrival(s, h, j).wait_recv()
                    core_copy(s, h, src).start()

                @pl.when(i == X + j)
                def _():
                    core_arrival(s, h, src).wait_recv()

            j = jnp.where(i < 2, 0, jnp.where(i <= X, i - 1, i - X))
            other = jnp.where(i < 2, i, jnp.where(i <= X, 0, 1))
            xi = lax.rem(mx - j + X, X)
            core = lax.rem(mc + other, 2)
            forward(s, h, xi * 2 + core)
            return 0

        lax.fori_loop(0, T, functools.partial(slice_step, 0), 0)
        pg, pu = pre_g[...], pre_u[...]
        sigma = jax.nn.sigmoid(pg)
        pre_u[...] = pu * sigma * (1.0 + pg * (1.0 - sigma))
        pre_g[...] = pg * sigma

        @pl.when(k == 0)
        def _():
            arrive(1, 1)

        lax.fori_loop(0, T, functools.partial(slice_step, 1), 0)

        @pl.when(k == E - 2)
        def _():
            arrive(k + 1, 1)

        gg[...] = (hid[...] * pre_u[...]).astype(BF16)
        ug[...] = (hid[...] * pre_g[...]).astype(BF16)

        def give(xi):
            a_send[s, xi] = part_of(xi * 2 + oc).astype(BF16)
            a_copy(s, xi).start()
            mine = part_of(xi * 2 + mc)
            a_copy(s, xi).wait_recv()
            return mine + a_recv[s, xi].astype(F32)

        def keep(j, _):
            b_send[s, j] = give(lax.rem(mx + j, X)).astype(BF16)
            for h in range(2):
                b_copy(s, j, h).start()
            return 0

        lax.fori_loop(1, X, keep, 0)
        @pl.when(k >= 1)
        def _():
            finish(nth(me, k - 1, E))

        own[s] = give(mx)

        @pl.when((k > 0) & (k < E - 2))
        def _():
            arrive(k + 1, 1)


        return 0

    lax.fori_loop(0, E, chunk, 0)
    finish(nth(me, E - 1, E))

    total = lax.dot_general(pt[me], c_send[me], TN, preferred_element_type=F32)
    for k in range(1, E):
        s = nth(me, k, E)
        for h in range(2):
            c_arrival(s, h).wait_recv()
        total = total + lax.dot_general(pt[s], c_recv[s], TN, preferred_element_type=F32)
    out_ref[...] = total.astype(BF16)

    def drain(s, _):
        for h in range(2):

            @pl.when(s != me)
            def _():
                z_copy(s, h).wait_send()
                c_copy(s, h).wait_send()

            for j in range(1, X):
                x_copy(s, h, j).wait_send()
                b_copy(s, j, h).wait_send()
            for xi in range(X):
                core_copy(s, h, xi).wait_send()
        for xi in range(X):
            a_copy(s, xi).wait_send()
        return 0

    lax.fori_loop(0, E, drain, 0)


def per_device(activations, out_grad, routes, gates, gate_weight, up_weight, down_weight):
    E = lax.axis_size("expert")
    T = lax.axis_size("tensor")
    X = T // 2
    tok, top = routes.shape
    W = activations.shape[1]
    D, FF = gate_weight.shape[1:]
    need = 3 * tok * top // (2 * E)
    cap = -(-need // 32) * 32
    vmem = pl.BlockSpec(memory_space=pltpu.VMEM)
    anywhere = pl.BlockSpec(memory_space=pl.ANY)
    dma = pltpu.SemaphoreType.DMA
    return pl.pallas_call(
        functools.partial(kernel, E, T, cap),
        out_shape=jax.ShapeDtypeStruct((tok, W), BF16),
        in_specs=[vmem] * 4 + [anywhere] * 3,
        out_specs=vmem,
        scratch_shapes=[
            pltpu.VMEM((D, FF), BF16),
            pltpu.VMEM((D, FF), BF16),
            pltpu.VMEM((FF, D), BF16),
            pltpu.VMEM((E, 2, cap, W), BF16),
            pltpu.VMEM((T, E, 2, cap, W), BF16),
            pltpu.VMEM((E, cap, tok), BF16),
            pltpu.VMEM((cap, FF), F32),
            pltpu.VMEM((cap, FF), F32),
            pltpu.VMEM((cap, FF), F32),
            pltpu.VMEM((cap, FF), BF16),
            pltpu.VMEM((cap, FF), BF16),
            pltpu.VMEM((E, cap, W), F32),
            pltpu.VMEM((E, X, cap, W), BF16),
            pltpu.VMEM((E, X, cap, W), BF16),
            pltpu.VMEM((E, X, cap, W), BF16),
            pltpu.VMEM((E, X, cap, W), BF16),
            pltpu.VMEM((E, cap, W), BF16),
            pltpu.VMEM((E, cap, W), BF16),
            dma((3,)),
            dma((2, E)), dma((2, E)),
            dma((2, X, E)), dma((2, X, E)),
            dma((2, X, E)), dma((2, X, E)),
            dma((X, E)), dma((X, E)),
            dma((2, X, E)), dma((2, X, E)),
            dma((2, E)), dma((2, E)),
        ],
        compiler_params=pltpu.CompilerParams(
            collective_id=0, has_side_effects=True, vmem_limit_bytes=62 * 1024 * 1024
        ),
        cost_estimate=pl.CostEstimate(
            flops=10 * E * cap * D * FF, bytes_accessed=6 * D * FF, transcendentals=E * cap * FF
        ),
    )(activations, out_grad, routes.T, gates.T, gate_weight[0], up_weight[0], down_weight[0])


def solution(mesh):
    return jax.shard_map(
        per_device,
        mesh=mesh,
        in_specs=(
            P(("group", "expert"), "tensor"),
            P(("group", "expert"), "tensor"),
            P(("group", "expert"), None),
            P(("group", "expert"), None),
            P("expert", None, "tensor"),
            P("expert", None, "tensor"),
            P("expert", "tensor", None),
        ),
        out_specs=P(("group", "expert"), "tensor"),
        check_vma=False,
    )
```
